32 devices in a mesh: ctx: 4 (over y, x), head: 8 (over z, core).
Axes of the slice: x: 2, y: 2, z: 4, core: 2. Of those that a mesh axis runs over, the one named last changes fastest.
Arguments:
- hidden_in: bfloat16 [4096, 5376], P(('ctx', 'head')), may hold values from -6 to 6
- pre_gain: float32 [5376], replicated, may hold values from 0.1 to 1.9
- w_query: bfloat16 [5376, 4096], P('ctx', 'head'), may hold values from -0.054554473 to 0.054554473, as said below
- w_key: bfloat16 [5376, 2048], P('ctx', 'head'), may hold values from -0.054554473 to 0.054554473, as said below
- value_weight: bfloat16 [5376, 2048], P('ctx', 'head'), may hold values from -0.078125 to 0.078125
- query_gain: float32 [128], replicated, may hold values from 0.6 to 7, as said below
- key_norm_gain: float32 [128], replicated, may hold values from 0.6 to 7, as said below
- w_output: bfloat16 [4096, 5376], P(('head', 'ctx')), may hold values from -0.09375 to 0.09375
- post_gain: float32 [5376], replicated, may hold values from 0.1 to 1.9
Outputs:
- layer_out: bfloat16 [4096, 5376], P(('ctx', 'head'))
The draws below stay inside these ranges and needn't reach their ends.
Inputs may be any that keep to these rules, and one draw needn't show every extreme that they name: `w_query`: entries are normal draws clipped to 4 standard deviations, scaled by 5376 ** -0.5. `w_key`: entries are normal draws clipped to 4 standard deviations, scaled by 5376 ** -0.5. `query_gain`: positive gains. `key_norm_gain`: positive gains.
All inputs are finite; a program needn't handle non-finite values.
Results may differ from the reference program's by a relative error of at most 0.015.
The reference program's roundings to bfloat16 on the way count: a program that leaves them out, or rounds other values in their place, can miss the bound.
Values may be sent and summed in bfloat16 or wider, within the bound.
A program may use at most 128 MiB of HBM per device.

```python
import jax
import jax.numpy as jnp
from jax import lax

MODEL_WIDTH = 5376
QUERY_HEADS = 32
KEY_VALUE_HEADS = 16
HEAD_SIZE = 128
WINDOW_SPAN = 1024
TOK_DEV = 1024
SLAB_TOKENS = 4096
N_HEAD = 8


def common_query(key):
    fresh_sample = jax.random.normal(jax.random.fold_in(key, 7), (MODEL_WIDTH, QUERY_HEADS * HEAD_SIZE), jnp.float32)
    return jnp.clip(fresh_sample, -4.0, 4.0) * MODEL_WIDTH ** (-0.5)


def draw_w_query(key, part):
    return common_query(key).astype(jnp.bfloat16)


def draw_w_key(key, part):
    fresh_sample = jax.random.normal(jax.random.fold_in(key, 8), (MODEL_WIDTH, KEY_VALUE_HEADS * HEAD_SIZE), jnp.float32)
    parent_sample = jnp.clip(fresh_sample, -4.0, 4.0) * MODEL_WIDTH ** (-0.5)
    return parent_sample.astype(jnp.bfloat16)


def gain_draw(key, salt):
    uniform_draw = jax.random.uniform(jax.random.fold_in(key, salt), (HEAD_SIZE,), jnp.float32)
    lower_end = jnp.log(0.6)
    upper_end = jnp.log(1.6)
    return jnp.exp(lower_end + uniform_draw * (upper_end - lower_end))


def draw_query_gain(key, part):
    return gain_draw(key, 21)


def draw_key_norm_gain(key, part):
    return gain_draw(key, 22)


def shard_levels(key, extent, shards, least, high):
    gain = 1.0
    for axis_at, shards_of in shards:
        draws = jax.random.uniform(jax.random.fold_in(jax.random.fold_in(key, 6), axis_at), (shards_of,), jnp.float32, least / len(shards), high / len(shards))
        gain = gain * jnp.repeat(jnp.exp(draws), extent[axis_at] // shards_of).reshape((-1,) + (1,) * (len(extent) - 1 - axis_at))
    return gain


def scatter_about(key, dims, spread, bound, split=(), kind=jnp.bfloat16):
    array = spread * jax.random.normal(key, dims, jnp.float32)
    if split:
        array = array * shard_levels(key, dims, split, -0.22, 0.18)
    return jnp.clip(array, -bound, bound).astype(kind)


def setup_inputs(seed: int = 0) -> dict:
    streams_of = jax.random.split(jax.random.key(seed), 10)
    hidden_in = scatter_about(streams_of[0], (SLAB_TOKENS, MODEL_WIDTH), 1.0, 6.0, ((0, 32),))
    pre_gain = jnp.clip(1.0 + 0.18 * jax.random.normal(streams_of[1], (MODEL_WIDTH,), jnp.float32), 0.1, 1.9)
    w_query = draw_w_query(jax.random.fold_in(streams_of[9], 71), 0)
    w_key = draw_w_key(jax.random.fold_in(streams_of[9], 71), 0)
    value_weight = scatter_about(streams_of[4], (MODEL_WIDTH, KEY_VALUE_HEADS * HEAD_SIZE), MODEL_WIDTH ** -0.5, 0.078125, ((0, 4), (1, 8)))
    query_gain = draw_query_gain(jax.random.fold_in(streams_of[9], 71), 0)
    key_norm_gain = draw_key_norm_gain(jax.random.fold_in(streams_of[9], 71), 0)
    w_output = scatter_about(streams_of[7], (QUERY_HEADS * HEAD_SIZE, MODEL_WIDTH), (QUERY_HEADS * HEAD_SIZE) ** -0.5, 0.09375, ((0, 32),))
    post_gain = jnp.clip(1.0 + 0.18 * jax.random.normal(streams_of[8], (MODEL_WIDTH,), jnp.float32), 0.1, 1.9)
    return dict(hidden_in=hidden_in, pre_gain=pre_gain, w_query=w_query, w_key=w_key, value_weight=value_weight, query_gain=query_gain, key_norm_gain=key_norm_gain, w_output=w_output, post_gain=post_gain)


norm_eps = 1e-06
query_scale = 168.0 ** (-0.5)
rope_base = 10000.0
mask_value = -1e+30

def root_mean_scale(values, scaling):
    mean_sq = lax.optimization_barrier(jnp.mean(values * values, axis=-1, keepdims=True))
    return values * lax.rsqrt(mean_sq + norm_eps) * scaling

def apply_rotary(values, token_places):
    full_width = values.shape[-1]
    half_width = full_width // 2
    frequency = rope_base ** (-jnp.arange(half_width, dtype=jnp.float32) * 2.0 / full_width)
    angles = token_places.astype(jnp.float32)[:, None] * frequency[None, :]
    cosine = jnp.cos(angles)[:, None, :]
    sine_part = jnp.sin(angles)[:, None, :]
    lower_half = values[..., :half_width]
    upper_half = values[..., half_width:]
    return jnp.concatenate([lower_half * cosine - upper_half * sine_part, upper_half * cosine + lower_half * sine_part], axis=-1)

def reference(hidden_in, pre_gain, w_query, w_key, value_weight, query_gain, key_norm_gain, w_output, post_gain):
    own_rows = hidden_in.astype(jnp.float32)
    normed = root_mean_scale(own_rows, pre_gain.astype(jnp.float32)).astype(jnp.bfloat16)
    query_raw = jnp.dot(normed, w_query, preferred_element_type=jnp.float32)
    key_unnormed = jnp.dot(normed, w_key, preferred_element_type=jnp.float32)
    value_unnormed = jnp.dot(normed, value_weight, preferred_element_type=jnp.float32)
    token_places = jnp.arange(SLAB_TOKENS, dtype=jnp.int32)
    query_matrix = (apply_rotary(root_mean_scale(query_raw.reshape(SLAB_TOKENS, QUERY_HEADS, HEAD_SIZE), query_gain.astype(jnp.float32)), token_places) * query_scale).astype(jnp.bfloat16)
    projected_keys = apply_rotary(root_mean_scale(key_unnormed.reshape(SLAB_TOKENS, KEY_VALUE_HEADS, HEAD_SIZE), key_norm_gain.astype(jnp.float32)), token_places).astype(jnp.bfloat16)
    projected_values = value_unnormed.astype(jnp.bfloat16).reshape(SLAB_TOKENS, KEY_VALUE_HEADS, HEAD_SIZE)
    heads_per_group = QUERY_HEADS // KEY_VALUE_HEADS
    block_rows = min(512, TOK_DEV)
    leading_zeros = jnp.zeros((WINDOW_SPAN, KEY_VALUE_HEADS, HEAD_SIZE), jnp.bfloat16)
    padded_keys = jnp.concatenate([leading_zeros, projected_keys], axis=0)
    padded_values = jnp.concatenate([leading_zeros, projected_values], axis=0)
    grouped_queries = query_matrix.reshape(SLAB_TOKENS, KEY_VALUE_HEADS, heads_per_group, HEAD_SIZE)

    def one_block(block_index):
        first_row = block_index * block_rows
        query_block = lax.dynamic_slice_in_dim(grouped_queries, first_row, block_rows, 0)
        key_block = lax.dynamic_slice_in_dim(padded_keys, first_row, block_rows + WINDOW_SPAN, 0)
        value_block = lax.dynamic_slice_in_dim(padded_values, first_row, block_rows + WINDOW_SPAN, 0)
        scores = jnp.einsum('qjgd,kjd->jgqk', query_block.astype(jnp.float32), key_block.astype(jnp.float32))
        query_spots = first_row + jnp.arange(block_rows, dtype=jnp.int32)
        key_spots = first_row - WINDOW_SPAN + jnp.arange(block_rows + WINDOW_SPAN, dtype=jnp.int32)
        allowed = (key_spots[None, :] <= query_spots[:, None]) & (key_spots[None, :] > query_spots[:, None] - WINDOW_SPAN) & (key_spots[None, :] >= 0)
        scores = jnp.where(allowed, scores, mask_value)
        row_max = lax.optimization_barrier(jnp.max(scores, axis=-1, keepdims=True))
        weights = jnp.exp(scores - row_max)
        row_sum = lax.optimization_barrier(jnp.sum(weights, axis=-1, keepdims=True))
        probabilities = (weights / row_sum).astype(jnp.bfloat16)
        mixed = jnp.einsum('jgqk,kjd->qjgd', probabilities.astype(jnp.float32), value_block.astype(jnp.float32))
        return mixed.astype(jnp.bfloat16).reshape(block_rows, QUERY_HEADS * HEAD_SIZE)
    attended = lax.map(one_block, jnp.arange(SLAB_TOKENS // block_rows, dtype=jnp.int32)).reshape(SLAB_TOKENS, QUERY_HEADS * HEAD_SIZE)
    group_width = QUERY_HEADS * HEAD_SIZE // N_HEAD

    def add_group(carried, group_index):
        columns = lax.dynamic_slice_in_dim(attended, group_index * group_width, group_width, 1)
        weight_rows = lax.dynamic_slice_in_dim(w_output, group_index * group_width, group_width, 0)
        partial_value = jnp.dot(columns, weight_rows, preferred_element_type=jnp.float32).astype(jnp.bfloat16)
        partial_value = lax.optimization_barrier(partial_value).astype(jnp.float32)
        return (carried + partial_value, None)
    summed, unused = lax.scan(add_group, jnp.zeros((SLAB_TOKENS, MODEL_WIDTH), jnp.float32), jnp.arange(N_HEAD, dtype=jnp.int32))
    return (own_rows + root_mean_scale(summed, post_gain.astype(jnp.float32))).astype(jnp.bfloat16)
```

```python
import jax
import jax.numpy as jnp
from jax import lax
from jax.experimental import pallas as pl
from jax.experimental.pallas import tpu as pltpu
from jax.sharding import PartitionSpec as P

HEAD_SIZE = 128
WINDOW_SPAN = 1024


norm_eps = 1e-06
query_scale = 168.0 ** (-0.5)
rope_base = 10000.0
mask_value = -1e30
COLUMN_TILE = 768
PIECES = 2


def ring_place(index, count):
    major, minor = index // 2, index % 2
    return major + minor * (count - 1 - 2 * major)


def ring_index(place, count):
    second = place // (count // 2)
    return (1 - second) * (2 * place) + second * (2 * (count - 1 - place) + 1)


def gather_kernel(
    count, chips, hidden, *refs
):
    shards, hidden_out, wholes = refs[:3], refs[3], refs[4:7]
    local_sem, head_send, head_recv, sib_send, sib_recv, ring_send, ring_recv = refs[7:]
    ctx = lax.axis_index("ctx")
    head = lax.axis_index("head")
    chip, core = head // 2, head % 2
    sibling = chip * 2 + 1 - core
    upper, lower = head + 2, head - 2
    has_upper, has_lower = chip < chips - 1, chip > 0
    place = ring_place(ctx, count)
    ahead = ring_index((place + 1) % count, count)
    behind = ring_index((place + count - 1) % count, count)
    rows = hidden.shape[0]

    barrier = pltpu.get_barrier_semaphore()
    pl.semaphore_signal(barrier, inc=1, device_id={"head": sibling})
    pl.semaphore_signal(barrier, inc=1, device_id={"ctx": ahead})
    pl.semaphore_signal(barrier, inc=1, device_id={"ctx": behind})

    @pl.when(has_upper)
    def _():
        pl.semaphore_signal(barrier, inc=1, device_id={"head": upper})

    @pl.when(has_lower)
    def _():
        pl.semaphore_signal(barrier, inc=1, device_id={"head": lower})

    pl.semaphore_wait(barrier, 3 + has_upper.astype(jnp.int32) + has_lower.astype(jnp.int32))

    def head_block(owner):
        return hidden_out.at[pl.ds(pl.multiple_of(owner * rows, rows), rows)]

    def chain_copy(way, distance, target, owner, source=None):
        block = head_block(owner)
        return pltpu.make_async_remote_copy(
            src_ref=block if source is None else source,
            dst_ref=block,
            send_sem=head_send.at[way, distance],
            recv_sem=head_recv.at[way, distance],
            device_id={"head": target},
        )

    def sibling_copy(owner, slot, source=None):
        block = head_block(owner)
        return pltpu.make_async_remote_copy(
            src_ref=block if source is None else source,
            dst_ref=block,
            send_sem=sib_send.at[slot],
            recv_sem=sib_recv.at[slot],
            device_id={"head": sibling},
        )

    def ring_copy(way, which, distance, half, target, owner, source=None):
        length = shards[which].shape[0]
        part = length // 2
        at = pl.multiple_of(owner * length + half * part, 16)
        block = wholes[which].at[pl.ds(at, part)]
        return pltpu.make_async_remote_copy(
            src_ref=block if source is None else shards[which].at[pl.ds(half * part, part)],
            dst_ref=block,
            send_sem=ring_send.at[way, which, distance, half],
            recv_sem=ring_recv.at[way, which, distance, half],
            device_id={"ctx": target},
        )

    @pl.when(has_upper)
    def _():
        chain_copy(0, 0, upper, head, hidden).start()

    @pl.when(has_lower)
    def _():
        chain_copy(1, 0, lower, head, hidden).start()

    targets = (ahead, behind)
    for which in range(3):
        for turn in range(2):
            for way in range(2):
                half = turn if way == 0 else 1 - turn
                ring_copy(way, which, 0, half, targets[way], ctx, True).start()
    sibling_copy(head, chip, hidden).start()
    own_copies = [pltpu.make_async_copy(hidden, head_block(head), local_sem.at[3])]
    for which in range(3):
        length = shards[which].shape[0]
        own_copies.append(
            pltpu.make_async_copy(
                shards[which],
                wholes[which].at[pl.ds(pl.multiple_of(ctx * length, 16), length)],
                local_sem.at[which],
            )
        )
    for copy in own_copies:
        copy.start()

    def head_step(distance):
        below = head - 2 * distance
        above = head + 2 * distance

        @pl.when(chip >= distance)
        def _():
            chain_copy(0, distance - 1, upper, below).wait_recv()

            @pl.when(has_upper)
            def _():
                if distance < chips - 1:
                    chain_copy(0, distance, upper, below).start()

            sibling_copy(below, chip - distance).start()

        @pl.when(chip + distance < chips)
        def _():
            chain_copy(1, distance - 1, lower, above).wait_recv()

            @pl.when(has_lower)
            def _():
                if distance < chips - 1:
                    chain_copy(1, distance, lower, above).start()

            sibling_copy(above, chip + distance).start()

    def ring_owner(way, distance):
        step = count - distance if way == 0 else distance
        return ring_index((place + step) % count, count)

    def ring_halves(distance, way):
        if distance == count // 2:
            return (0,) if way == 0 else (1,)
        return (0, 1) if way == 0 else (1, 0)

    def ring_step(distance):
        for which in range(3):
            for turn in range(2):
                for way in range(2):
                    halves = ring_halves(distance, way)
                    if turn >= len(halves):
                        continue
                    half = halves[turn]
                    owner = ring_owner(way, distance)
                    ring_copy(way, which, distance - 1, half, targets[way], owner).wait_recv()
                    if distance < count // 2 and half in ring_halves(distance + 1, way):
                        ring_copy(way, which, distance, half, targets[way], owner).start()

    for distance in range(1, max(chips, count // 2 + 1)):
        if distance < chips:
            head_step(distance)
        if distance <= count // 2:
            ring_step(distance)

    for other in range(chips):
        sibling_copy(other * 2 + 1 - core, other).wait_recv()
    for copy in own_copies:
        copy.wait()
    for other in range(chips):
        sibling_copy(other * 2 + core, other).wait_send()
    for distance in range(chips - 1):
        @pl.when(has_upper & (chip >= distance))
        def _():
            chain_copy(0, distance, upper, head - 2 * distance).wait_send()

        @pl.when(has_lower & (chip + distance < chips))
        def _():
            chain_copy(1, distance, lower, head + 2 * distance).wait_send()

    for distance in range(count // 2):
        for which in range(3):
            for way in range(2):
                for half in ring_halves(distance + 1, way):
                    ring_copy(
                        way, which, distance, half, targets[way], ring_owner(way, distance)
                    ).wait_send()


def gather_all(hidden_in, w_query, w_key, value_weight):
    count = lax.axis_size("ctx")
    chips = lax.axis_size("head") // 2
    any_spec = pl.BlockSpec(memory_space=pl.ANY)

    def grown(shard, times):
        return jax.ShapeDtypeStruct((shard.shape[0] * times, shard.shape[1]), shard.dtype)

    dma = pltpu.SemaphoreType.DMA
    return pl.pallas_call(
        lambda *refs: gather_kernel(count, chips, *refs),
        out_shape=(
            grown(hidden_in, 2 * chips),
            grown(w_query, count),
            grown(w_key, count),
            grown(value_weight, count),
        ),
        in_specs=[any_spec] * 4,
        out_specs=(any_spec,) * 4,
        scratch_shapes=[
            dma((4,)),
            dma((2, chips)),
            dma((2, chips)),
            dma((chips,)),
            dma((chips,)),
            dma((2, 3, count // 2, 2)),
            dma((2, 3, count // 2, 2)),
        ],
        compiler_params=pltpu.CompilerParams(
            collective_id=0, has_side_effects=True, vmem_limit_bytes=4 * 2**20
        ),
    )(hidden_in, w_query, w_key, value_weight)


def scatter_kernel(
    chips,
    attended,
    weight,
    out,
    part,
    pair_in,
    down_in,
    up_in,
    pair_send,
    pair_recv,
    chain_send,
    chain_recv,
):
    head = lax.axis_index("head")
    chip, core = head // 2, head % 2
    sibling = chip * 2 + 1 - core
    upper, lower = head + 2, head - 2
    has_upper, has_lower = chip < chips - 1, chip > 0
    rows = out.shape[0]
    width = out.shape[1]
    piece = rows // PIECES
    tiles = width // COLUMN_TILE
    mine = pl.multiple_of(core * rows, rows)

    barrier = pltpu.get_barrier_semaphore()
    pl.semaphore_signal(barrier, inc=1, device_id={"head": sibling})

    @pl.when(has_upper)
    def _():
        pl.semaphore_signal(barrier, inc=1, device_id={"head": upper})

    @pl.when(has_lower)
    def _():
        pl.semaphore_signal(barrier, inc=1, device_id={"head": lower})

    pl.semaphore_wait(barrier, 1 + has_upper.astype(jnp.int32) + has_lower.astype(jnp.int32))

    def pair_copy(target):
        return pltpu.make_async_remote_copy(
            src_ref=part.at[target, pl.ds(pl.multiple_of((1 - core) * rows, rows), rows)],
            dst_ref=pair_in.at[target],
            send_sem=pair_send.at[target],
            recv_sem=pair_recv.at[target],
            device_id={"head": sibling},
        )

    landing = (up_in, down_in)

    def chain_copy(way, target, at):
        return pltpu.make_async_remote_copy(
            src_ref=part.at[target, pl.ds(pl.multiple_of(mine + at * piece, piece), piece)],
            dst_ref=landing[way].at[target, pl.ds(at * piece, piece)],
            send_sem=chain_send.at[way, target, at],
            recv_sem=chain_recv.at[way, target, at],
            device_id={"head": upper if way == 0 else lower},
        )

    def project(target):
        start = pl.multiple_of(target * 2 * rows, 2 * rows)

        @pl.loop(0, tiles)
        def _(tile):
            columns = pl.ds(pl.multiple_of(tile * COLUMN_TILE, COLUMN_TILE), COLUMN_TILE)
            part[target, :, columns] = jnp.dot(
                attended[pl.ds(start, 2 * rows), :],
                weight[:, columns],
                preferred_element_type=jnp.float32,
            ).astype(jnp.bfloat16)

        pair_copy(target).start()

    def targets_at(step):
        return step + chip - (chips - 1), chips - 1 - step + chip

    def compute(step):
        if step == chips - 1:
            project(chip)
        elif step < chips - 1:
            down, up = targets_at(step)

            @pl.when(down >= 0)
            def _():
                project(down)

            @pl.when(up < chips)
            def _():
                project(up)

    def add_into(way, target, at, with_chain):
        spot = pl.ds(pl.multiple_of(mine + at * piece, piece), piece)
        near = pl.ds(at * piece, piece)

        @pl.loop(0, tiles)
        def _(tile):
            columns = pl.ds(pl.multiple_of(tile * COLUMN_TILE, COLUMN_TILE), COLUMN_TILE)
            value = part[target, spot, columns].astype(jnp.float32)
            value += pair_in[target, near, columns].astype(jnp.float32)
            if with_chain:
                value += landing[way][target, near, columns].astype(jnp.float32)
            part[target, spot, columns] = value.astype(jnp.bfloat16)

    def relay(way, target):
        source_there = has_lower if way == 0 else has_upper
        pair_copy(target).wait_recv()
        for at in range(PIECES):
            @pl.when(source_there)
            def _():
                chain_copy(way, target, at).wait_recv()
                add_into(way, target, at, True)

            @pl.when(jnp.logical_not(source_there))
            def _():
                add_into(way, target, at, False)

            chain_copy(way, target, at).start()

    compute(0)
    compute(1)
    for step in range(chips - 1):
        down, up = targets_at(step)

        @pl.when(down >= 0)
        def _():
            relay(1, down)

        @pl.when(up < chips)
        def _():
            relay(0, up)

        compute(step + 2)

    pair_copy(chip).wait_recv()

    @pl.loop(0, tiles)
    def _(tile):
        columns = pl.ds(pl.multiple_of(tile * COLUMN_TILE, COLUMN_TILE), COLUMN_TILE)
        out[:, columns] = part[chip, pl.ds(mine, rows), columns].astype(jnp.float32) + pair_in[
            chip, :, columns
        ].astype(jnp.float32)

    for way, there in ((0, has_lower), (1, has_upper)):
        @pl.when(there)
        def _():
            for at in range(PIECES):
                chain_copy(way, chip, at).wait_recv()

            @pl.loop(0, tiles)
            def _(tile):
                columns = pl.ds(pl.multiple_of(tile * COLUMN_TILE, COLUMN_TILE), COLUMN_TILE)
                out[:, columns] += landing[way][chip, :, columns].astype(jnp.float32)

    for target in range(chips):
        pair_copy(target).wait_send()

    for step in range(chips - 1):
        for way, target in ((1, step + chip - (chips - 1)), (0, chips - 1 - step + chip)):
            @pl.when((target >= 0) & (target < chips))
            def _():
                for at in range(PIECES):
                    chain_copy(way, target, at).wait_send()


def project_and_scatter(attended, out_weight):
    chips = lax.axis_size("head") // 2
    rows = attended.shape[0] // (2 * chips)
    width = out_weight.shape[1]
    dma = pltpu.SemaphoreType.DMA
    return pl.pallas_call(
        lambda *refs: scatter_kernel(chips, *refs),
        out_shape=jax.ShapeDtypeStruct((rows, width), jnp.float32),
        in_specs=[pl.BlockSpec(memory_space=pltpu.VMEM)] * 2,
        out_specs=pl.BlockSpec(memory_space=pltpu.VMEM),
        scratch_shapes=[
            pltpu.VMEM((chips, 2 * rows, width), jnp.bfloat16),
            pltpu.VMEM((chips, rows, width), jnp.bfloat16),
            pltpu.VMEM((chips, rows, width), jnp.bfloat16),
            pltpu.VMEM((chips, rows, width), jnp.bfloat16),
            dma((chips,)),
            dma((chips,)),
            dma((2, chips, PIECES)),
            dma((2, chips, PIECES)),
        ],
        compiler_params=pltpu.CompilerParams(
            collective_id=1, has_side_effects=True, vmem_limit_bytes=54 * 2**20
        ),
    )(attended, out_weight)


def passed_along(shard, axis, by):
    count = lax.axis_size(axis)
    pairs = [(i, i + by) for i in range(count) if 0 <= i + by < count]
    return lax.ppermute(shard, axis, pairs)


def root_mean_scale(values, scaling):
    mean_sq = jnp.mean(values * values, axis=-1, keepdims=True)
    return values * lax.rsqrt(mean_sq + norm_eps) * scaling


def apply_rotary(values, token_places):
    full_width = values.shape[-1]
    half_width = full_width // 2
    frequency = rope_base ** (-jnp.arange(half_width, dtype=jnp.float32) * 2.0 / full_width)
    angles = token_places.astype(jnp.float32)[:, None] * frequency[None, :]
    cosine = jnp.cos(angles)[:, None, :]
    sine_part = jnp.sin(angles)[:, None, :]
    lower_half = values[..., :half_width]
    upper_half = values[..., half_width:]
    return jnp.concatenate(
        [
            lower_half * cosine - upper_half * sine_part,
            upper_half * cosine + lower_half * sine_part,
        ],
        axis=-1,
    )


def body(
    hidden_in,
    pre_gain,
    w_query,
    w_key,
    value_weight,
    query_gain,
    key_norm_gain,
    w_output,
    post_gain,
):
    own_rows = hidden_in.astype(jnp.float32)
    raw_rows, whole_query, whole_key, whole_value = gather_all(
        hidden_in, w_query, w_key, value_weight
    )
    w_output, raw_rows = lax.optimization_barrier((w_output, raw_rows))
    out_weight = lax.all_gather(w_output, "ctx", axis=0, tiled=True)
    normed = root_mean_scale(raw_rows.astype(jnp.float32), pre_gain).astype(jnp.bfloat16)
    tok_count = normed.shape[0]

    def add_rows(weight):
        return jnp.dot(normed, weight, preferred_element_type=jnp.float32)

    query_raw = add_rows(whole_query)
    key_unnormed = add_rows(whole_key)
    value_unnormed = add_rows(whole_value)
    local_heads = w_query.shape[1] // HEAD_SIZE
    local_groups = w_key.shape[1] // HEAD_SIZE
    heads_per_group = local_heads // local_groups
    ctx_index = lax.axis_index("ctx")
    token_places = ctx_index * tok_count + jnp.arange(tok_count, dtype=jnp.int32)
    query_matrix = (
        apply_rotary(
            root_mean_scale(query_raw.reshape(tok_count, local_heads, HEAD_SIZE), query_gain),
            token_places,
        )
        * query_scale
    ).astype(jnp.bfloat16)
    projected_keys = apply_rotary(
        root_mean_scale(key_unnormed.reshape(tok_count, local_groups, HEAD_SIZE), key_norm_gain),
        token_places,
    ).astype(jnp.bfloat16)
    projected_values = value_unnormed.astype(jnp.bfloat16)
    key_value = jnp.stack(
        [projected_keys.reshape(tok_count, local_groups * HEAD_SIZE), projected_values]
    )
    pieces = [passed_along(key_value, "ctx", 1)]
    extended = jnp.concatenate(pieces + [key_value], axis=1)
    band_keys = extended[0].reshape(-1, local_groups, HEAD_SIZE)
    band_values = extended[1].reshape(-1, local_groups, HEAD_SIZE)
    block_rows = min(512, tok_count)
    grouped_queries = query_matrix.reshape(tok_count, local_groups, heads_per_group, HEAD_SIZE)
    outputs = []
    for block_index in range(tok_count // block_rows):
        first_row = block_index * block_rows
        query_block = grouped_queries[first_row : first_row + block_rows]
        key_block = band_keys[first_row : first_row + block_rows + WINDOW_SPAN]
        value_block = band_values[first_row : first_row + block_rows + WINDOW_SPAN]
        scores = jnp.einsum(
            "qjgd,kjd->jgqk", query_block, key_block, preferred_element_type=jnp.float32
        )
        query_spots = token_places[first_row : first_row + block_rows]
        key_spots = (
            ctx_index * tok_count
            - WINDOW_SPAN
            + first_row
            + jnp.arange(block_rows + WINDOW_SPAN, dtype=jnp.int32)
        )
        allowed = (
            (key_spots[None, :] <= query_spots[:, None])
            & (key_spots[None, :] > query_spots[:, None] - WINDOW_SPAN)
            & (key_spots[None, :] >= 0)
        )
        scores = jnp.where(allowed, scores, mask_value)
        row_max = jnp.max(scores, axis=-1, keepdims=True)
        weights = jnp.exp(scores - row_max)
        row_sum = jnp.sum(weights, axis=-1, keepdims=True)
        probabilities = (weights / row_sum).astype(jnp.bfloat16)
        mixed = jnp.einsum(
            "jgqk,kjd->qjgd", probabilities, value_block, preferred_element_type=jnp.float32
        )
        outputs.append(mixed.astype(jnp.bfloat16).reshape(block_rows, local_heads * HEAD_SIZE))
    attended = jnp.concatenate(outputs, axis=0)
    summed = project_and_scatter(attended, out_weight)
    result = own_rows + root_mean_scale(summed, post_gain)
    return result.astype(jnp.bfloat16)


def solution(mesh):
    return jax.shard_map(
        body,
        mesh=mesh,
        in_specs=(
            P(("ctx", "head"), None),
            P(),
            P("ctx", "head"),
            P("ctx", "head"),
            P("ctx", "head"),
            P(),
            P(),
            P(("head", "ctx"), None),
            P(),
        ),
        out_specs=P(("ctx", "head"), None),
        check_vma=False,
    )
```

```python
import jax
import jax.numpy as jnp
from jax import lax
from jax.experimental import pallas as pl
from jax.experimental.pallas import tpu as pltpu
from jax.sharding import PartitionSpec as P

HEAD_SIZE = 128
WINDOW_SPAN = 1024


norm_eps = 1e-06
query_scale = 168.0 ** (-0.5)
rope_base = 10000.0
mask_value = -1e30
COLUMN_TILE = 768
PIECES = 2


def ring_place(index, count):
    major, minor = index // 2, index % 2
    return major + minor * (count - 1 - 2 * major)


def ring_index(place, count):
    second = place // (count // 2)
    return (1 - second) * (2 * place) + second * (2 * (count - 1 - place) + 1)


def gather_kernel(
    count, chips, hidden, *refs
):
    shards, hidden_out, wholes = refs[:3], refs[3], refs[4:7]
    local_sem, head_send, head_recv, sib_send, sib_recv, ring_send, ring_recv = refs[7:]
    ctx = lax.axis_index("ctx")
    head = lax.axis_index("head")
    chip, core = head // 2, head % 2
    sibling = chip * 2 + 1 - core
    upper, lower = head + 2, head - 2
    has_upper, has_lower = chip < chips - 1, chip > 0
    place = ring_place(ctx, count)
    ahead = ring_index((place + 1) % count, count)
    behind = ring_index((place + count - 1) % count, count)
    rows = hidden.shape[0]

    barrier = pltpu.get_barrier_semaphore()
    pl.semaphore_signal(barrier, inc=1, device_id={"head": sibling})
    pl.semaphore_signal(barrier, inc=1, device_id={"ctx": ahead})
    pl.semaphore_signal(barrier, inc=1, device_id={"ctx": behind})

    @pl.when(has_upper)
    def _():
        pl.semaphore_signal(barrier, inc=1, device_id={"head": upper})

    @pl.when(has_lower)
    def _():
        pl.semaphore_signal(barrier, inc=1, device_id={"head": lower})

    pl.semaphore_wait(barrier, 3 + has_upper.astype(jnp.int32) + has_lower.astype(jnp.int32))

    def head_block(owner):
        return hidden_out.at[pl.ds(pl.multiple_of(owner * rows, rows), rows)]

    def chain_copy(way, distance, target, owner, source=None):
        block = head_block(owner)
        return pltpu.make_async_remote_copy(
            src_ref=block if source is None else source,
            dst_ref=block,
            send_sem=head_send.at[way, distance],
            recv_sem=head_recv.at[way, distance],
            device_id={"head": target},
        )

    def sibling_copy(owner, slot, source=None):
        block = head_block(owner)
        return pltpu.make_async_remote_copy(
            src_ref=block if source is None else source,
            dst_ref=block,
            send_sem=sib_send.at[slot],
            recv_sem=sib_recv.at[slot],
            device_id={"head": sibling},
        )

    def ring_copy(way, which, distance, half, target, owner, source=None):
        length = shards[which].shape[0]
        part = length // 2
        at = pl.multiple_of(owner * length + half * part, 16)
        block = wholes[which].at[pl.ds(at, part)]
        return pltpu.make_async_remote_copy(
            src_ref=block if source is None else shards[which].at[pl.ds(half * part, part)],
            dst_ref=block,
            send_sem=ring_send.at[way, which, distance, half],
            recv_sem=ring_recv.at[way, which, distance, half],
            device_id={"ctx": target},
        )

    @pl.when(has_upper)
    def _():
        chain_copy(0, 0, upper, head, hidden).start()

    @pl.when(has_lower)
    def _():
        chain_copy(1, 0, lower, head, hidden).start()

    targets = (ahead, behind)
    for which in range(3):
        for turn in range(2):
            for way in range(2):
                half = turn if way == 0 else 1 - turn
                ring_copy(way, which, 0, half, targets[way], ctx, True).start()
    sibling_copy(head, chip, hidden).start()
    own_copies = [pltpu.make_async_copy(hidden, head_block(head), local_sem.at[3])]
    for which in range(3):
        length = shards[which].shape[0]
        own_copies.append(
            pltpu.make_async_copy(
                shards[which],
                wholes[which].at[pl.ds(pl.multiple_of(ctx * length, 16), length)],
                local_sem.at[which],
            )
        )
    for copy in own_copies:
        copy.start()

    def head_step(distance):
        below = head - 2 * distance
        above = head + 2 * distance

        @pl.when(chip >= distance)
        def _():
            chain_copy(0, distance - 1, upper, below).wait_recv()

            @pl.when(has_upper)
            def _():
                if distance < chips - 1:
                    chain_copy(0, distance, upper, below).start()

            sibling_copy(below, chip - distance).start()

        @pl.when(chip + distance < chips)
        def _():
            chain_copy(1, distance - 1, lower, above).wait_recv()

            @pl.when(has_lower)
            def _():
                if distance < chips - 1:
                    chain_copy(1, distance, lower, above).start()

            sibling_copy(above, chip + distance).start()

    def ring_owner(way, distance):
        step = count - distance if way == 0 else distance
        return ring_index((place + step) % count, count)

    def ring_halves(distance, way):
        if distance == count // 2:
            return (0,) if way == 0 else (1,)
        return (0, 1) if way == 0 else (1, 0)

    def ring_step(distance):
        for which in range(3):
            for turn in range(2):
                for way in range(2):
                    halves = ring_halves(distance, way)
                    if turn >= len(halves):
                        continue
                    half = halves[turn]
                    owner = ring_owner(way, distance)
                    ring_copy(way, which, distance - 1, half, targets[way], owner).wait_recv()
                    if distance < count // 2 and half in ring_halves(distance + 1, way):
                        ring_copy(way, which, distance, half, targets[way], owner).start()

    for distance in range(1, max(chips, count // 2 + 1)):
        if distance < chips:
            head_step(distance)
        if distance <= count // 2:
            ring_step(distance)

    for other in range(chips):
        sibling_copy(other * 2 + 1 - core, other).wait_recv()
    for copy in own_copies:
        copy.wait()
    for other in range(chips):
        sibling_copy(other * 2 + core, other).wait_send()
    for distance in range(chips - 1):
        @pl.when(has_upper & (chip >= distance))
        def _():
            chain_copy(0, distance, upper, head - 2 * distance).wait_send()

        @pl.when(has_lower & (chip + distance < chips))
        def _():
            chain_copy(1, distance, lower, head + 2 * distance).wait_send()

    for distance in range(count // 2):
        for which in range(3):
            for way in range(2):
                for half in ring_halves(distance + 1, way):
                    ring_copy(
                        way, which, distance, half, targets[way], ring_owner(way, distance)
                    ).wait_send()


def gather_all(hidden_in, w_query, w_key, value_weight):
    count = lax.axis_size("ctx")
    chips = lax.axis_size("head") // 2
    any_spec = pl.BlockSpec(memory_space=pl.ANY)

    def grown(shard, times):
        return jax.ShapeDtypeStruct((shard.shape[0] * times, shard.shape[1]), shard.dtype)

    dma = pltpu.SemaphoreType.DMA
    return pl.pallas_call(
        lambda *refs: gather_kernel(count, chips, *refs),
        out_shape=(
            grown(hidden_in, 2 * chips),
            grown(w_query, count),
            grown(w_key, count),
            grown(value_weight, count),
        ),
        in_specs=[any_spec] * 4,
        out_specs=(any_spec,) * 4,
        scratch_shapes=[
            dma((4,)),
            dma((2, chips)),
            dma((2, chips)),
            dma((chips,)),
            dma((chips,)),
            dma((2, 3, count // 2, 2)),
            dma((2, 3, count // 2, 2)),
        ],
        compiler_params=pltpu.CompilerParams(
            collective_id=0, has_side_effects=True, vmem_limit_bytes=54 * 2**20
        ),
    )(hidden_in, w_query, w_key, value_weight)


def scatter_kernel(
    chips,
    attended,
    weight,
    out,
    part,
    pair_in,
    down_in,
    up_in,
    pair_send,
    pair_recv,
    chain_send,
    chain_recv,
):
    head = lax.axis_index("head")
    chip, core = head // 2, head % 2
    sibling = chip * 2 + 1 - core
    upper, lower = head + 2, head - 2
    has_upper, has_lower = chip < chips - 1, chip > 0
    rows = out.shape[0]
    width = out.shape[1]
    piece = rows // PIECES
    tiles = width // COLUMN_TILE
    mine = pl.multiple_of(core * rows, rows)

    barrier = pltpu.get_barrier_semaphore()
    pl.semaphore_signal(barrier, inc=1, device_id={"head": sibling})

    @pl.when(has_upper)
    def _():
        pl.semaphore_signal(barrier, inc=1, device_id={"head": upper})

    @pl.when(has_lower)
    def _():
        pl.semaphore_signal(barrier, inc=1, device_id={"head": lower})

    pl.semaphore_wait(barrier, 1 + has_upper.astype(jnp.int32) + has_lower.astype(jnp.int32))

    def pair_copy(target):
        return pltpu.make_async_remote_copy(
            src_ref=part.at[target, pl.ds(pl.multiple_of((1 - core) * rows, rows), rows)],
            dst_ref=pair_in.at[target],
            send_sem=pair_send.at[target],
            recv_sem=pair_recv.at[target],
            device_id={"head": sibling},
        )

    landing = (up_in, down_in)

    def chain_copy(way, target, at):
        return pltpu.make_async_remote_copy(
            src_ref=part.at[target, pl.ds(pl.multiple_of(mine + at * piece, piece), piece)],
            dst_ref=landing[way].at[target, pl.ds(at * piece, piece)],
            send_sem=chain_send.at[way, target, at],
            recv_sem=chain_recv.at[way, target, at],
            device_id={"head": upper if way == 0 else lower},
        )

    def project(target):
        start = pl.multiple_of(target * 2 * rows, 2 * rows)

        @pl.loop(0, tiles)
        def _(tile):
            columns = pl.ds(pl.multiple_of(tile * COLUMN_TILE, COLUMN_TILE), COLUMN_TILE)
            part[target, :, columns] = jnp.dot(
                attended[pl.ds(start, 2 * rows), :],
                weight[:, columns],
                preferred_element_type=jnp.float32,
            ).astype(jnp.bfloat16)

        pair_copy(target).start()

    def targets_at(step):
        return step + chip - (chips - 1), chips - 1 - step + chip

    def compute(step):
        if step == chips - 1:
            project(chip)
        elif step < chips - 1:
            down, up = targets_at(step)

            @pl.when(down >= 0)
            def _():
                project(down)

            @pl.when(up < chips)
            def _():
                project(up)

    def add_into(way, target, at, with_chain):
        spot = pl.ds(pl.multiple_of(mine + at * piece, piece), piece)
        near = pl.ds(at * piece, piece)

        @pl.loop(0, tiles)
        def _(tile):
            columns = pl.ds(pl.multiple_of(tile * COLUMN_TILE, COLUMN_TILE), COLUMN_TILE)
            value = part[target, spot, columns].astype(jnp.float32)
            value += pair_in[target, near, columns].astype(jnp.float32)
            if with_chain:
                value += landing[way][target, near, columns].astype(jnp.float32)
            part[target, spot, columns] = value.astype(jnp.bfloat16)

    def relay(way, target):
        source_there = has_lower if way == 0 else has_upper
        pair_copy(target).wait_recv()
        for at in range(PIECES):
            @pl.when(source_there)
            def _():
                chain_copy(way, target, at).wait_recv()
                add_into(way, target, at, True)

            @pl.when(jnp.logical_not(source_there))
            def _():
                add_into(way, target, at, False)

            chain_copy(way, target, at).start()

    compute(0)
    compute(1)
    for step in range(chips - 1):
        down, up = targets_at(step)

        @pl.when(down >= 0)
        def _():
            relay(1, down)

        @pl.when(up < chips)
        def _():
            relay(0, up)

        compute(step + 2)

    pair_copy(chip).wait_recv()

    @pl.loop(0, tiles)
    def _(tile):
        columns = pl.ds(pl.multiple_of(tile * COLUMN_TILE, COLUMN_TILE), COLUMN_TILE)
        out[:, columns] = part[chip, pl.ds(mine, rows), columns].astype(jnp.float32) + pair_in[
            chip, :, columns
        ].astype(jnp.float32)

    for way, there in ((0, has_lower), (1, has_upper)):
        @pl.when(there)
        def _():
            for at in range(PIECES):
                chain_copy(way, chip, at).wait_recv()

            @pl.loop(0, tiles)
            def _(tile):
                columns = pl.ds(pl.multiple_of(tile * COLUMN_TILE, COLUMN_TILE), COLUMN_TILE)
                out[:, columns] += landing[way][chip, :, columns].astype(jnp.float32)

    for target in range(chips):
        pair_copy(target).wait_send()

    for step in range(chips - 1):
        for way, target in ((1, step + chip - (chips - 1)), (0, chips - 1 - step + chip)):
            @pl.when((target >= 0) & (target < chips))
            def _():
                for at in range(PIECES):
                    chain_copy(way, target, at).wait_send()


def project_and_scatter(attended, out_weight):
    chips = lax.axis_size("head") // 2
    rows = attended.shape[0] // (2 * chips)
    width = out_weight.shape[1]
    dma = pltpu.SemaphoreType.DMA
    return pl.pallas_call(
        lambda *refs: scatter_kernel(chips, *refs),
        out_shape=jax.ShapeDtypeStruct((rows, width), jnp.float32),
        in_specs=[pl.BlockSpec(memory_space=pltpu.VMEM)] * 2,
        out_specs=pl.BlockSpec(memory_space=pltpu.VMEM),
        scratch_shapes=[
            pltpu.VMEM((chips, 2 * rows, width), jnp.bfloat16),
            pltpu.VMEM((chips, rows, width), jnp.bfloat16),
            pltpu.VMEM((chips, rows, width), jnp.bfloat16),
            pltpu.VMEM((chips, rows, width), jnp.bfloat16),
            dma((chips,)),
            dma((chips,)),
            dma((2, chips, PIECES)),
            dma((2, chips, PIECES)),
        ],
        compiler_params=pltpu.CompilerParams(
            collective_id=1, has_side_effects=True, vmem_limit_bytes=54 * 2**20
        ),
    )(attended, out_weight)


def passed_along(shard, axis, by):
    count = lax.axis_size(axis)
    pairs = [(i, i + by) for i in range(count) if 0 <= i + by < count]
    return lax.ppermute(shard, axis, pairs)


def root_mean_scale(values, scaling):
    mean_sq = jnp.mean(values * values, axis=-1, keepdims=True)
    return values * lax.rsqrt(mean_sq + norm_eps) * scaling


def apply_rotary(values, token_places):
    full_width = values.shape[-1]
    half_width = full_width // 2
    frequency = rope_base ** (-jnp.arange(half_width, dtype=jnp.float32) * 2.0 / full_width)
    angles = token_places.astype(jnp.float32)[:, None] * frequency[None, :]
    cosine = jnp.cos(angles)[:, None, :]
    sine_part = jnp.sin(angles)[:, None, :]
    lower_half = values[..., :half_width]
    upper_half = values[..., half_width:]
    return jnp.concatenate(
        [
            lower_half * cosine - upper_half * sine_part,
            upper_half * cosine + lower_half * sine_part,
        ],
        axis=-1,
    )


def body(
    hidden_in,
    pre_gain,
    w_query,
    w_key,
    value_weight,
    query_gain,
    key_norm_gain,
    w_output,
    post_gain,
):
    own_rows = hidden_in.astype(jnp.float32)
    raw_rows, whole_query, whole_key, whole_value = gather_all(
        hidden_in, w_query, w_key, value_weight
    )
    w_output, raw_rows = lax.optimization_barrier((w_output, raw_rows))
    out_weight = lax.all_gather(w_output, "ctx", axis=0, tiled=True)
    normed = root_mean_scale(raw_rows.astype(jnp.float32), pre_gain).astype(jnp.bfloat16)
    tok_count = normed.shape[0]

    def add_rows(weight):
        return jnp.dot(normed, weight, preferred_element_type=jnp.float32)

    query_raw = add_rows(whole_query)
    key_unnormed = add_rows(whole_key)
    value_unnormed = add_rows(whole_value)
    local_heads = w_query.shape[1] // HEAD_SIZE
    local_groups = w_key.shape[1] // HEAD_SIZE
    heads_per_group = local_heads // local_groups
    ctx_index = lax.axis_index("ctx")
    token_places = ctx_index * tok_count + jnp.arange(tok_count, dtype=jnp.int32)
    query_matrix = (
        apply_rotary(
            root_mean_scale(query_raw.reshape(tok_count, local_heads, HEAD_SIZE), query_gain),
            token_places,
        )
        * query_scale
    ).astype(jnp.bfloat16)
    projected_keys = apply_rotary(
        root_mean_scale(key_unnormed.reshape(tok_count, local_groups, HEAD_SIZE), key_norm_gain),
        token_places,
    ).astype(jnp.bfloat16)
    projected_values = value_unnormed.astype(jnp.bfloat16)
    key_value = jnp.stack(
        [projected_keys.reshape(tok_count, local_groups * HEAD_SIZE), projected_values]
    )
    earlier = passed_along(key_value, "ctx", 1)
    own_keys, own_values = (projected_keys, projected_values.reshape(projected_keys.shape))
    past_keys = earlier[0].reshape(-1, local_groups, HEAD_SIZE)
    past_values = earlier[1].reshape(-1, local_groups, HEAD_SIZE)
    block_rows = min(512, tok_count)
    grouped_queries = query_matrix.reshape(tok_count, local_groups, heads_per_group, HEAD_SIZE)

    def masked_scores(query_block, first_row, keys, first_key):
        scores = jnp.einsum("qjgd,kjd->jgqk", query_block, keys, preferred_element_type=jnp.float32)
        query_spots = token_places[first_row : first_row + block_rows]
        key_spots = (
            ctx_index * tok_count + first_key + jnp.arange(keys.shape[0], dtype=jnp.int32)
        )
        allowed = (
            (key_spots[None, :] <= query_spots[:, None])
            & (key_spots[None, :] > query_spots[:, None] - WINDOW_SPAN)
            & (key_spots[None, :] >= 0)
        )
        return jnp.where(allowed, scores, mask_value)

    def weigh(weights, values):
        return jnp.einsum(
            "jgqk,kjd->jgqd",
            weights.astype(jnp.bfloat16),
            values,
            preferred_element_type=jnp.float32,
        )

    own_parts = []
    for first_row in range(0, tok_count, block_rows):
        last_row = first_row + block_rows
        scores = masked_scores(
            grouped_queries[first_row:last_row], first_row, own_keys[:last_row], 0
        )
        own_max = jnp.max(scores, axis=-1, keepdims=True)
        weights = jnp.exp(scores - own_max)
        own_sum = jnp.sum(weights, axis=-1, keepdims=True)
        own_parts.append((own_max, own_sum, weigh(weights, own_values[:last_row])))
    outputs = []
    for block_index, (own_max, own_sum, own_mixed) in enumerate(own_parts):
        first_row = block_index * block_rows
        from_row = tok_count - WINDOW_SPAN + first_row
        scores = masked_scores(
            grouped_queries[first_row : first_row + block_rows],
            first_row,
            past_keys[from_row:],
            from_row - tok_count,
        )
        row_max = jnp.maximum(own_max, jnp.max(scores, axis=-1, keepdims=True))
        weights = jnp.exp(scores - row_max)
        rescale = jnp.exp(own_max - row_max)
        row_sum = own_sum * rescale + jnp.sum(weights, axis=-1, keepdims=True)
        mixed = (own_mixed * rescale + weigh(weights, past_values[from_row:])) / row_sum
        mixed = mixed.astype(jnp.bfloat16).transpose(2, 0, 1, 3)
        outputs.append(mixed.reshape(block_rows, local_heads * HEAD_SIZE))
    attended = jnp.concatenate(outputs, axis=0)
    summed = project_and_scatter(attended, out_weight)
    result = own_rows + root_mean_scale(summed, post_gain)
    return result.astype(jnp.bfloat16)


def solution(mesh):
    return jax.shard_map(
        body,
        mesh=mesh,
        in_specs=(
            P(("ctx", "head"), None),
            P(),
            P("ctx", "head"),
            P("ctx", "head"),
            P("ctx", "head"),
            P(),
            P(),
            P(("head", "ctx"), None),
            P(),
        ),
        out_specs=P(("ctx", "head"), None),
        check_vma=False,
    )
```

```python
import jax
import jax.numpy as jnp
from jax import lax
from jax.experimental import pallas as pl
from jax.experimental.pallas import tpu as pltpu
from jax.sharding import PartitionSpec as P

HEAD_SIZE = 128
WINDOW_SPAN = 1024


norm_eps = 1e-06
query_scale = 168.0 ** (-0.5)
rope_base = 10000.0
mask_value = -1e30
COLUMN_TILE = 768
PIECES = 2


def ring_place(index, count):
    major, minor = index // 2, index % 2
    return major + minor * (count - 1 - 2 * major)


def ring_index(place, count):
    second = place // (count // 2)
    return (1 - second) * (2 * place) + second * (2 * (count - 1 - place) + 1)


def gather_kernel(
    count, chips, hidden, *refs
):
    shards, hidden_out, wholes = refs[:3], refs[3], refs[4:7]
    local_sem, head_send, head_recv, sib_send, sib_recv, ring_send, ring_recv = refs[7:]
    ctx = lax.axis_index("ctx")
    head = lax.axis_index("head")
    chip, core = head // 2, head % 2
    sibling = chip * 2 + 1 - core
    upper, lower = head + 2, head - 2
    has_upper, has_lower = chip < chips - 1, chip > 0
    place = ring_place(ctx, count)
    ahead = ring_index((place + 1) % count, count)
    behind = ring_index((place + count - 1) % count, count)
    rows = hidden.shape[0]

    barrier = pltpu.get_barrier_semaphore()
    pl.semaphore_signal(barrier, inc=1, device_id={"head": sibling})
    pl.semaphore_signal(barrier, inc=1, device_id={"ctx": ahead})
    pl.semaphore_signal(barrier, inc=1, device_id={"ctx": behind})

    @pl.when(has_upper)
    def _():
        pl.semaphore_signal(barrier, inc=1, device_id={"head": upper})

    @pl.when(has_lower)
    def _():
        pl.semaphore_signal(barrier, inc=1, device_id={"head": lower})

    pl.semaphore_wait(barrier, 3 + has_upper.astype(jnp.int32) + has_lower.astype(jnp.int32))

    def head_block(owner):
        return hidden_out.at[pl.ds(pl.multiple_of(owner * rows, rows), rows)]

    def chain_copy(way, distance, target, owner, source=None):
        block = head_block(owner)
        return pltpu.make_async_remote_copy(
            src_ref=block if source is None else source,
            dst_ref=block,
            send_sem=head_send.at[way, distance],
            recv_sem=head_recv.at[way, distance],
            device_id={"head": target},
        )

    def sibling_copy(owner, slot, source=None):
        block = head_block(owner)
        return pltpu.make_async_remote_copy(
            src_ref=block if source is None else source,
            dst_ref=block,
            send_sem=sib_send.at[slot],
            recv_sem=sib_recv.at[slot],
            device_id={"head": sibling},
        )

    def ring_copy(way, which, distance, half, target, owner, source=None):
        length = shards[which].shape[0]
        part = length // 2
        at = pl.multiple_of(owner * length + half * part, 16)
        block = wholes[which].at[pl.ds(at, part)]
        return pltpu.make_async_remote_copy(
            src_ref=block if source is None else shards[which].at[pl.ds(half * part, part)],
            dst_ref=block,
            send_sem=ring_send.at[way, which, distance, half],
            recv_sem=ring_recv.at[way, which, distance, half],
            device_id={"ctx": target},
        )

    @pl.when(has_upper)
    def _():
        chain_copy(0, 0, upper, head, hidden).start()

    @pl.when(has_lower)
    def _():
        chain_copy(1, 0, lower, head, hidden).start()

    targets = (ahead, behind)
    for which in range(3):
        for turn in range(2):
            for way in range(2):
                half = turn if way == 0 else 1 - turn
                ring_copy(way, which, 0, half, targets[way], ctx, True).start()
    sibling_copy(head, chip, hidden).start()
    own_copies = [pltpu.make_async_copy(hidden, head_block(head), local_sem.at[3])]
    for which in range(3):
        length = shards[which].shape[0]
        own_copies.append(
            pltpu.make_async_copy(
                shards[which],
                wholes[which].at[pl.ds(pl.multiple_of(ctx * length, 16), length)],
                local_sem.at[which],
            )
        )
    for copy in own_copies:
        copy.start()

    def head_step(distance):
        below = head - 2 * distance
        above = head + 2 * distance

        @pl.when(chip >= distance)
        def _():
            chain_copy(0, distance - 1, upper, below).wait_recv()

            @pl.when(has_upper)
            def _():
                if distance < chips - 1:
                    chain_copy(0, distance, upper, below).start()

            sibling_copy(below, chip - distance).start()

        @pl.when(chip + distance < chips)
        def _():
            chain_copy(1, distance - 1, lower, above).wait_recv()

            @pl.when(has_lower)
            def _():
                if distance < chips - 1:
                    chain_copy(1, distance, lower, above).start()

            sibling_copy(above, chip + distance).start()

    def ring_owner(way, distance):
        step = count - distance if way == 0 else distance
        return ring_index((place + step) % count, count)

    def ring_halves(distance, way):
        if distance == count // 2:
            return (0,) if way == 0 else (1,)
        return (0, 1) if way == 0 else (1, 0)

    def ring_step(distance):
        for which in range(3):
            for turn in range(2):
                for way in range(2):
                    halves = ring_halves(distance, way)
                    if turn >= len(halves):
                        continue
                    half = halves[turn]
                    owner = ring_owner(way, distance)
                    ring_copy(way, which, distance - 1, half, targets[way], owner).wait_recv()
                    if distance < count // 2 and half in ring_halves(distance + 1, way):
                        ring_copy(way, which, distance, half, targets[way], owner).start()

    for distance in range(1, max(chips, count // 2 + 1)):
        if distance < chips:
            head_step(distance)
        if distance <= count // 2:
            ring_step(distance)

    for other in range(chips):
        sibling_copy(other * 2 + 1 - core, other).wait_recv()
    for copy in own_copies:
        copy.wait()
    for other in range(chips):
        sibling_copy(other * 2 + core, other).wait_send()
    for distance in range(chips - 1):
        @pl.when(has_upper & (chip >= distance))
        def _():
            chain_copy(0, distance, upper, head - 2 * distance).wait_send()

        @pl.when(has_lower & (chip + distance < chips))
        def _():
            chain_copy(1, distance, lower, head + 2 * distance).wait_send()

    for distance in range(count // 2):
        for which in range(3):
            for way in range(2):
                for half in ring_halves(distance + 1, way):
                    ring_copy(
                        way, which, distance, half, targets[way], ring_owner(way, distance)
                    ).wait_send()


def gather_all(hidden_in, w_query, w_key, value_weight):
    count = lax.axis_size("ctx")
    chips = lax.axis_size("head") // 2
    any_spec = pl.BlockSpec(memory_space=pl.ANY)

    def grown(shard, times):
        return jax.ShapeDtypeStruct((shard.shape[0] * times, shard.shape[1]), shard.dtype)

    dma = pltpu.SemaphoreType.DMA
    return pl.pallas_call(
        lambda *refs: gather_kernel(count, chips, *refs),
        out_shape=(
            grown(hidden_in, 2 * chips),
            grown(w_query, count),
            grown(w_key, count),
            grown(value_weight, count),
        ),
        in_specs=[any_spec] * 4,
        out_specs=(any_spec,) * 4,
        scratch_shapes=[
            dma((4,)),
            dma((2, chips)),
            dma((2, chips)),
            dma((chips,)),
            dma((chips,)),
            dma((2, 3, count // 2, 2)),
            dma((2, 3, count // 2, 2)),
        ],
        compiler_params=pltpu.CompilerParams(
            collective_id=0, has_side_effects=True, vmem_limit_bytes=4 * 2**20
        ),
    )(hidden_in, w_query, w_key, value_weight)


def scatter_kernel(
    chips,
    attended,
    weight,
    out,
    part,
    pair_in,
    down_in,
    up_in,
    pair_send,
    pair_recv,
    chain_send,
    chain_recv,
):
    head = lax.axis_index("head")
    chip, core = head // 2, head % 2
    sibling = chip * 2 + 1 - core
    upper, lower = head + 2, head - 2
    has_upper, has_lower = chip < chips - 1, chip > 0
    rows = out.shape[0]
    width = out.shape[1]
    piece = rows // PIECES
    tiles = width // COLUMN_TILE
    mine = pl.multiple_of(core * rows, rows)

    barrier = pltpu.get_barrier_semaphore()
    pl.semaphore_signal(barrier, inc=1, device_id={"head": sibling})

    @pl.when(has_upper)
    def _():
        pl.semaphore_signal(barrier, inc=1, device_id={"head": upper})

    @pl.when(has_lower)
    def _():
        pl.semaphore_signal(barrier, inc=1, device_id={"head": lower})

    pl.semaphore_wait(barrier, 1 + has_upper.astype(jnp.int32) + has_lower.astype(jnp.int32))

    def pair_copy(target):
        return pltpu.make_async_remote_copy(
            src_ref=part.at[target, pl.ds(pl.multiple_of((1 - core) * rows, rows), rows)],
            dst_ref=pair_in.at[target],
            send_sem=pair_send.at[target],
            recv_sem=pair_recv.at[target],
            device_id={"head": sibling},
        )

    landing = (up_in, down_in)

    def chain_copy(way, target, at):
        return pltpu.make_async_remote_copy(
            src_ref=part.at[target, pl.ds(pl.multiple_of(mine + at * piece, piece), piece)],
            dst_ref=landing[way].at[target, pl.ds(at * piece, piece)],
            send_sem=chain_send.at[way, target, at],
            recv_sem=chain_recv.at[way, target, at],
            device_id={"head": upper if way == 0 else lower},
        )

    def project(target):
        start = pl.multiple_of(target * 2 * rows, 2 * rows)

        @pl.loop(0, tiles)
        def _(tile):
            columns = pl.ds(pl.multiple_of(tile * COLUMN_TILE, COLUMN_TILE), COLUMN_TILE)
            part[target, :, columns] = jnp.dot(
                attended[pl.ds(start, 2 * rows), :],
                weight[:, columns],
                preferred_element_type=jnp.float32,
            ).astype(jnp.bfloat16)

        pair_copy(target).start()

    def targets_at(step):
        return step + chip - (chips - 1), chips - 1 - step + chip

    def compute(step):
        if step == chips - 1:
            project(chip)
        elif step < chips - 1:
            down, up = targets_at(step)

            @pl.when(down >= 0)
            def _():
                project(down)

            @pl.when(up < chips)
            def _():
                project(up)

    def add_into(way, target, at, with_chain):
        spot = pl.ds(pl.multiple_of(mine + at * piece, piece), piece)
        near = pl.ds(at * piece, piece)

        @pl.loop(0, tiles)
        def _(tile):
            columns = pl.ds(pl.multiple_of(tile * COLUMN_TILE, COLUMN_TILE), COLUMN_TILE)
            value = part[target, spot, columns].astype(jnp.float32)
            value += pair_in[target, near, columns].astype(jnp.float32)
            if with_chain:
                value += landing[way][target, near, columns].astype(jnp.float32)
            part[target, spot, columns] = value.astype(jnp.bfloat16)

    def relay(way, target):
        source_there = has_lower if way == 0 else has_upper
        pair_copy(target).wait_recv()
        for at in range(PIECES):
            @pl.when(source_there)
            def _():
                chain_copy(way, target, at).wait_recv()
                add_into(way, target, at, True)

            @pl.when(jnp.logical_not(source_there))
            def _():
                add_into(way, target, at, False)

            chain_copy(way, target, at).start()

    compute(0)
    compute(1)
    for step in range(chips - 1):
        down, up = targets_at(step)

        @pl.when(down >= 0)
        def _():
            relay(1, down)

        @pl.when(up < chips)
        def _():
            relay(0, up)

        compute(step + 2)

    pair_copy(chip).wait_recv()

    @pl.loop(0, tiles)
    def _(tile):
        columns = pl.ds(pl.multiple_of(tile * COLUMN_TILE, COLUMN_TILE), COLUMN_TILE)
        out[:, columns] = part[chip, pl.ds(mine, rows), columns].astype(jnp.float32) + pair_in[
            chip, :, columns
        ].astype(jnp.float32)

    for way, there in ((0, has_lower), (1, has_upper)):
        @pl.when(there)
        def _():
            for at in range(PIECES):
                chain_copy(way, chip, at).wait_recv()

            @pl.loop(0, tiles)
            def _(tile):
                columns = pl.ds(pl.multiple_of(tile * COLUMN_TILE, COLUMN_TILE), COLUMN_TILE)
                out[:, columns] += landing[way][chip, :, columns].astype(jnp.float32)

    for target in range(chips):
        pair_copy(target).wait_send()

    for step in range(chips - 1):
        for way, target in ((1, step + chip - (chips - 1)), (0, chips - 1 - step + chip)):
            @pl.when((target >= 0) & (target < chips))
            def _():
                for at in range(PIECES):
                    chain_copy(way, target, at).wait_send()


def project_and_scatter(attended, out_weight):
    chips = lax.axis_size("head") // 2
    rows = attended.shape[0] // (2 * chips)
    width = out_weight.shape[1]
    dma = pltpu.SemaphoreType.DMA
    return pl.pallas_call(
        lambda *refs: scatter_kernel(chips, *refs),
        out_shape=jax.ShapeDtypeStruct((rows, width), jnp.float32),
        in_specs=[pl.BlockSpec(memory_space=pltpu.VMEM)] * 2,
        out_specs=pl.BlockSpec(memory_space=pltpu.VMEM),
        scratch_shapes=[
            pltpu.VMEM((chips, 2 * rows, width), jnp.bfloat16),
            pltpu.VMEM((chips, rows, width), jnp.bfloat16),
            pltpu.VMEM((chips, rows, width), jnp.bfloat16),
            pltpu.VMEM((chips, rows, width), jnp.bfloat16),
            dma((chips,)),
            dma((chips,)),
            dma((2, chips, PIECES)),
            dma((2, chips, PIECES)),
        ],
        compiler_params=pltpu.CompilerParams(
            collective_id=1, has_side_effects=True, vmem_limit_bytes=54 * 2**20
        ),
    )(attended, out_weight)


def passed_along(shard, axis, by):
    count = lax.axis_size(axis)
    pairs = [(i, i + by) for i in range(count) if 0 <= i + by < count]
    return lax.ppermute(shard, axis, pairs)


def root_mean_scale(values, scaling):
    mean_sq = jnp.mean(values * values, axis=-1, keepdims=True)
    return values * lax.rsqrt(mean_sq + norm_eps) * scaling


def apply_rotary(values, token_places):
    full_width = values.shape[-1]
    half_width = full_width // 2
    frequency = rope_base ** (-jnp.arange(half_width, dtype=jnp.float32) * 2.0 / full_width)
    angles = token_places.astype(jnp.float32)[:, None] * frequency[None, :]
    cosine = jnp.cos(angles)[:, None, :]
    sine_part = jnp.sin(angles)[:, None, :]
    lower_half = values[..., :half_width]
    upper_half = values[..., half_width:]
    return jnp.concatenate(
        [
            lower_half * cosine - upper_half * sine_part,
            upper_half * cosine + lower_half * sine_part,
        ],
        axis=-1,
    )


def body(
    hidden_in,
    pre_gain,
    w_query,
    w_key,
    value_weight,
    query_gain,
    key_norm_gain,
    w_output,
    post_gain,
):
    own_rows = hidden_in.astype(jnp.float32)
    raw_rows, whole_query, whole_key, whole_value = gather_all(
        hidden_in, w_query, w_key, value_weight
    )
    out_weight = lax.all_gather(w_output, "ctx", axis=0, tiled=True)
    normed = root_mean_scale(raw_rows.astype(jnp.float32), pre_gain).astype(jnp.bfloat16)
    tok_count = normed.shape[0]

    def add_rows(weight):
        return jnp.dot(normed, weight, preferred_element_type=jnp.float32)

    query_raw = add_rows(whole_query)
    key_unnormed = add_rows(whole_key)
    value_unnormed = add_rows(whole_value)
    local_heads = w_query.shape[1] // HEAD_SIZE
    local_groups = w_key.shape[1] // HEAD_SIZE
    heads_per_group = local_heads // local_groups
    ctx_index = lax.axis_index("ctx")
    token_places = ctx_index * tok_count + jnp.arange(tok_count, dtype=jnp.int32)
    query_matrix = (
        apply_rotary(
            root_mean_scale(query_raw.reshape(tok_count, local_heads, HEAD_SIZE), query_gain),
            token_places,
        )
        * query_scale
    ).astype(jnp.bfloat16)
    projected_keys = apply_rotary(
        root_mean_scale(key_unnormed.reshape(tok_count, local_groups, HEAD_SIZE), key_norm_gain),
        token_places,
    ).astype(jnp.bfloat16)
    projected_values = value_unnormed.astype(jnp.bfloat16)
    key_value = jnp.stack(
        [projected_keys.reshape(tok_count, local_groups * HEAD_SIZE), projected_values]
    )
    earlier = passed_along(key_value, "ctx", 1)
    own_keys, own_values = (projected_keys, projected_values.reshape(projected_keys.shape))
    past_keys = earlier[0].reshape(-1, local_groups, HEAD_SIZE)
    past_values = earlier[1].reshape(-1, local_groups, HEAD_SIZE)
    block_rows = min(512, tok_count)
    grouped_queries = query_matrix.reshape(tok_count, local_groups, heads_per_group, HEAD_SIZE)

    def masked_scores(query_block, first_row, keys, first_key):
        scores = jnp.einsum("qjgd,kjd->jgqk", query_block, keys, preferred_element_type=jnp.float32)
        query_spots = token_places[first_row : first_row + block_rows]
        key_spots = (
            ctx_index * tok_count + first_key + jnp.arange(keys.shape[0], dtype=jnp.int32)
        )
        allowed = (
            (key_spots[None, :] <= query_spots[:, None])
            & (key_spots[None, :] > query_spots[:, None] - WINDOW_SPAN)
            & (key_spots[None, :] >= 0)
        )
        return jnp.where(allowed, scores, mask_value)

    def weigh(weights, values):
        return jnp.einsum(
            "jgqk,kjd->jgqd",
            weights.astype(jnp.bfloat16),
            values,
            preferred_element_type=jnp.float32,
        )

    own_parts = []
    for first_row in range(0, tok_count, block_rows):
        last_row = first_row + block_rows
        scores = masked_scores(
            grouped_queries[first_row:last_row], first_row, own_keys[:last_row], 0
        )
        own_max = jnp.max(scores, axis=-1, keepdims=True)
        weights = jnp.exp(scores - own_max)
        own_sum = jnp.sum(weights, axis=-1, keepdims=True)
        own_parts.append((own_max, own_sum, weigh(weights, own_values[:last_row])))
    outputs = []
    for block_index, (own_max, own_sum, own_mixed) in enumerate(own_parts):
        first_row = block_index * block_rows
        from_row = tok_count - WINDOW_SPAN + first_row
        scores = masked_scores(
            grouped_queries[first_row : first_row + block_rows],
            first_row,
            past_keys[from_row:],
            from_row - tok_count,
        )
        row_max = jnp.maximum(own_max, jnp.max(scores, axis=-1, keepdims=True))
        weights = jnp.exp(scores - row_max)
        rescale = jnp.exp(own_max - row_max)
        row_sum = own_sum * rescale + jnp.sum(weights, axis=-1, keepdims=True)
        mixed = (own_mixed * rescale + weigh(weights, past_values[from_row:])) / row_sum
        mixed = mixed.astype(jnp.bfloat16).transpose(2, 0, 1, 3)
        outputs.append(mixed.reshape(block_rows, local_heads * HEAD_SIZE))
    attended = jnp.concatenate(outputs, axis=0)
    summed = project_and_scatter(attended, out_weight)
    result = own_rows + root_mean_scale(summed, post_gain)
    return result.astype(jnp.bfloat16)


def solution(mesh):
    return jax.shard_map(
        body,
        mesh=mesh,
        in_specs=(
            P(("ctx", "head"), None),
            P(),
            P("ctx", "head"),
            P("ctx", "head"),
            P("ctx", "head"),
            P(),
            P(),
            P(("head", "ctx"), None),
            P(),
        ),
        out_specs=P(("ctx", "head"), None),
        check_vma=False,
    )
```
